512 devices in a mesh: rows: 64 (over y_lo, z, x), protos: 8 (over y_hi, core).
Axes of the slice: x: 4, y: 8 (y_hi: 4, y_lo: 2; y = y_hi * 2 + y_lo), z: 8, core: 2. Of those that a mesh axis runs over, the one named last changes fastest.
Arguments:
- embeddings: bfloat16 [65536, 1024], P('rows'), may hold values from -6 to 6
- prototypes: bfloat16 [8192, 1024], P('protos'), may hold values from -6 to 6
Outputs:
- codes: bfloat16 [65536, 8192], P('rows', 'protos')
- centers: bfloat16 [8192, 1024], P('protos')
The draws below stay inside these ranges and needn't reach their ends.
All inputs are finite; a program needn't handle non-finite values.
Results may differ from the reference program's by a relative error of at most 0.004.
Values may be sent and summed in bfloat16 or wider, within the bound.
No kernel may reach another device: no remote copies, remote signals or barrier semaphores. Data moves between devices by JAX's collectives and lax.ppermute only.
A program may use at most 64 MiB of HBM per device.

```python
import jax
import jax.numpy as jnp
from jax import lax

D = 1024
K = 8192
ITERS = 3
R_DEV = 1024
TOTAL_ROWS = 65536


latent_groups = 16


def latent_directions(key):
    return jax.random.normal(key, (latent_groups, D), jnp.float32)


def draw_embeddings(key, part):
    directions = latent_directions(key)
    key = jax.random.fold_in(key, 11)
    subkeys = jax.random.split(key, 4)
    block_count = TOTAL_ROWS // R_DEV
    home_latent = jax.random.randint(subkeys[0], (block_count,), 0, latent_groups)
    offset_draw = jax.random.randint(subkeys[1], (TOTAL_ROWS,), 0, 2 * latent_groups)
    offset = jnp.where(offset_draw < latent_groups, 0, offset_draw - latent_groups)
    row_block = jnp.arange(TOTAL_ROWS, dtype=jnp.int32) // R_DEV
    latent_index = (home_latent[row_block] + offset) % latent_groups
    strength = jax.random.uniform(subkeys[2], (TOTAL_ROWS, 1), jnp.float32, 0.45, 0.85)
    row_noise = jax.random.normal(subkeys[3], (TOTAL_ROWS, D), jnp.float32)
    values = strength * directions[latent_index] + row_noise
    return jnp.clip(values, -6.0, 6.0).astype(jnp.bfloat16)


def draw_prototypes(key, part):
    directions = latent_directions(key)
    key = jax.random.fold_in(key, 23)
    subkeys = jax.random.split(key, 2)
    group_index = jnp.arange(K, dtype=jnp.int32) * latent_groups // K
    strength = jax.random.uniform(subkeys[0], (K, 1), jnp.float32, 0.45, 0.85)
    proto_noise = jax.random.normal(subkeys[1], (K, D), jnp.float32)
    values = strength * directions[group_index] + proto_noise
    return jnp.clip(values, -6.0, 6.0).astype(jnp.bfloat16)


def setup_inputs(seed: int = 0) -> dict:
    arg_keys = jax.random.split(jax.random.key(seed), 3)
    return {
        "embeddings": draw_embeddings(jax.random.fold_in(arg_keys[2], 71), 0),
        "prototypes": draw_prototypes(jax.random.fold_in(arg_keys[2], 71), 0),
    }


def unit_norm(values):
    wide = values.astype(jnp.float32)
    total = lax.optimization_barrier(jnp.sum(wide * wide, axis=1, keepdims=True))
    return (wide / jnp.sqrt(total + 1e-06)).astype(jnp.bfloat16)

def reference(embeddings, prototypes):
    unit_rows = unit_norm(embeddings)
    unit_protos = unit_norm(prototypes)
    kernel = jnp.exp(jnp.dot(unit_rows, unit_protos.T, preferred_element_type=jnp.float32) / 0.05)
    row_scale = jnp.ones((TOTAL_ROWS,), jnp.float32)
    col_scale = jnp.ones((K,), jnp.float32)
    for step in range(ITERS):
        col_scale = 1.0 / (K * lax.optimization_barrier(jnp.sum(kernel * row_scale[:, None], axis=0)))
        row_scale = 1.0 / (TOTAL_ROWS * lax.optimization_barrier(jnp.sum(kernel * col_scale[None, :], axis=1)))
    codes = (float(TOTAL_ROWS) * float(K) * row_scale[:, None] * kernel * col_scale[None, :]).astype(jnp.bfloat16)
    sums = jnp.dot(codes.T, embeddings, preferred_element_type=jnp.float32)
    mean_square = lax.optimization_barrier(jnp.mean(sums * sums, axis=1, keepdims=True))
    centers = (sums / jnp.sqrt(mean_square + 1e-06)).astype(jnp.bfloat16)
    return (codes, centers)
```

```python
import jax
import jax.numpy as jnp
from jax import lax
from jax.sharding import Mesh, PartitionSpec as P

ITERS = 3
ROWS = ("ylo", "zhi", "zlo", "x")
PROTOS = ("yhi", "core")
NEAR = ("ylo", "zlo", "x")
FAR = ("zhi",)
SIZES = {"ylo": 2, "zhi": 4, "zlo": 2, "x": 4, "yhi": 4, "core": 2}


def count(axes):
    total = 1
    for axis in axes:
        total *= SIZES[axis]
    return total


def exchange(blocks, axes):
    return lax.all_to_all(blocks, axes, 0, 0, tiled=True)


def everyone(block, axes):
    return exchange(jnp.broadcast_to(block[None], (count(axes), *block.shape)), axes)


def sum_small(vector, axes):
    return jnp.sum(everyone(vector.reshape(-1, 128), axes), axis=0).reshape(vector.shape)


def scatter_sum(blocks, axes):
    count_ = count(axes)
    split = blocks.reshape(count_, blocks.shape[0] // count_, blocks.shape[1])
    return jnp.sum(exchange(split.astype(jnp.bfloat16), axes).astype(jnp.float32), axis=0)


def gather(block, axes):
    return everyone(block, axes).reshape(-1, block.shape[-1])


def unit_norm(values):
    wide = values.astype(jnp.float32)
    total = jnp.sum(wide * wide, axis=1, keepdims=True)
    return (wide / jnp.sqrt(total + 1e-06)).astype(jnp.bfloat16)


def body(embeddings, prototypes):
    row_count = embeddings.shape[0] * count(ROWS)
    proto_count = prototypes.shape[0] * count(PROTOS)
    unit_rows = unit_norm(embeddings)
    unit_protos = unit_norm(prototypes)
    kernel = jnp.exp(jnp.dot(unit_rows, unit_protos.T, preferred_element_type=jnp.float32) / 0.05)
    row_scale = jnp.ones((embeddings.shape[0],), jnp.float32)
    for step in range(ITERS):
        col_part = jnp.sum(kernel * row_scale[:, None], axis=0)
        col_scale = 1.0 / (proto_count * sum_small(col_part, ROWS))
        row_part = jnp.sum(kernel * col_scale[None, :], axis=1)
        row_scale = 1.0 / (row_count * sum_small(row_part, PROTOS))
    codes = (
        float(row_count) * float(proto_count) * row_scale[:, None] * kernel * col_scale[None, :]
    ).astype(jnp.bfloat16)
    feature_width = embeddings.shape[1]
    term = lax.dot_general(
        codes, embeddings, (((0,), (0,)), ((), ())), preferred_element_type=jnp.float32
    )
    sums = scatter_sum(scatter_sum(term, NEAR), FAR)
    squares = jnp.sum(sums * sums, axis=1, keepdims=True)
    scaled = (sums / jnp.sqrt(squares / feature_width + 1e-06)).astype(jnp.bfloat16)
    centers = gather(gather(scaled, FAR), NEAR)
    return (codes, centers)


def solution(mesh):
    fine = Mesh(mesh.devices.reshape(tuple(SIZES.values())), tuple(SIZES))
    return jax.shard_map(
        body,
        mesh=fine,
        in_specs=(P(ROWS, None), P(PROTOS, None)),
        out_specs=(P(ROWS, PROTOS), P(PROTOS, None)),
        check_vma=False,
    )
```

```python
import functools

import jax
import jax.numpy as jnp
from jax import lax
from jax.experimental import pallas as pl
from jax.experimental.pallas import tpu as pltpu
from jax.sharding import Mesh, PartitionSpec as P

ITERS = 3
LANES = 128
ROWS = ("ylo", "zhi", "zlo", "x")
PROTOS = ("yhi", "core")
NEAR = ("ylo", "zlo", "x")
FAR = ("zhi",)
SIZES = {"ylo": 2, "zhi": 4, "zlo": 2, "x": 4, "yhi": 4, "core": 2}


def count(axes):
    total = 1
    for axis in axes:
        total *= SIZES[axis]
    return total


def exchange(blocks, axes):
    return lax.all_to_all(blocks, axes, 0, 0, tiled=True)


def everyone(block, axes):
    return exchange(jnp.broadcast_to(block[None], (count(axes), *block.shape)), axes)


def on_chip(body, out_shape, operands, flops, moved):
    spec = pl.BlockSpec(memory_space=pltpu.VMEM)
    return pl.pallas_call(
        body,
        out_shape=out_shape,
        in_specs=[spec] * len(operands),
        out_specs=jax.tree.map(lambda _: spec, out_shape),
        compiler_params=pltpu.CompilerParams(vmem_limit_bytes=40 * 1024 * 1024),
        cost_estimate=pl.CostEstimate(flops=flops, bytes_accessed=moved, transcendentals=0),
    )(*operands)


def blocks_of(size):
    return [slice(start, start + LANES) for start in range(0, size, LANES)]


def down_rows(line):
    return jnp.broadcast_to(line, (LANES, LANES)).T


def row_body(scale, kernel_ref, parts_ref, col_ref, out_ref):
    col_scale = 1.0 / (scale * jnp.sum(parts_ref[...], axis=0))
    col_ref[...] = col_scale
    lines = []
    for rows in blocks_of(kernel_ref.shape[0]):
        total = None
        for k, lanes in enumerate(blocks_of(kernel_ref.shape[1])):
            tile = kernel_ref[rows, lanes] * col_scale[k : k + 1, :]
            total = tile if total is None else total + tile
        lines.append(jnp.sum(total.T, axis=0, keepdims=True))
    out_ref[...] = jnp.broadcast_to(jnp.concatenate(lines, axis=0)[None], out_ref.shape)


def col_body(scale, kernel_ref, parts_ref, out_ref):
    row_scale = 1.0 / (scale * jnp.sum(parts_ref[...], axis=0))
    totals = [None] * (kernel_ref.shape[1] // LANES)
    for r, rows in enumerate(blocks_of(kernel_ref.shape[0])):
        turned = down_rows(row_scale[r : r + 1, :])
        for k, lanes in enumerate(blocks_of(kernel_ref.shape[1])):
            tile = kernel_ref[rows, lanes] * turned
            part = jnp.sum(tile.reshape(LANES // 8, 8, LANES), axis=0)
            totals[k] = part if totals[k] is None else totals[k] + part
    lines = [jnp.sum(total, axis=0, keepdims=True) for total in totals]
    out_ref[...] = jnp.broadcast_to(jnp.concatenate(lines, axis=0)[None], out_ref.shape)


def codes_body(scale, mass, kernel_ref, parts_ref, col_ref, codes_ref):
    row_scale = mass / (scale * jnp.sum(parts_ref[...], axis=0))
    col_scale = col_ref[...]
    for r, rows in enumerate(blocks_of(kernel_ref.shape[0])):
        turned = down_rows(row_scale[r : r + 1, :])
        for k, lanes in enumerate(blocks_of(kernel_ref.shape[1])):
            tile = turned * kernel_ref[rows, lanes] * col_scale[k : k + 1, :]
            codes_ref[rows, lanes] = tile.astype(jnp.bfloat16)


def unit_norm(values):
    wide = values.astype(jnp.float32)
    total = jnp.sum(wide * wide, axis=1, keepdims=True)
    return (wide / jnp.sqrt(total + 1e-06)).astype(jnp.bfloat16)


def body(embeddings, prototypes):
    rows, protos = embeddings.shape[0], prototypes.shape[0]
    row_count = float(rows * count(ROWS))
    proto_count = float(protos * count(PROTOS))
    unit_rows = unit_norm(embeddings)
    unit_protos = unit_norm(prototypes)
    kernel = jnp.exp(jnp.dot(unit_rows, unit_protos.T, preferred_element_type=jnp.float32) / 0.05)
    line_rows = jax.ShapeDtypeStruct((rows // LANES, LANES), jnp.float32)
    line_protos = jax.ShapeDtypeStruct((protos // LANES, LANES), jnp.float32)
    copies_rows = jax.ShapeDtypeStruct((count(PROTOS), *line_rows.shape), jnp.float32)
    copies_protos = jax.ShapeDtypeStruct((count(ROWS), *line_protos.shape), jnp.float32)
    work = 2 * rows * protos
    col_parts = everyone(jnp.sum(kernel, axis=0).reshape(line_protos.shape), ROWS)
    for step in range(ITERS):
        col_scale, row_sums = on_chip(
            functools.partial(row_body, proto_count),
            (line_protos, copies_rows),
            (kernel, col_parts),
            work,
            2 * work,
        )
        row_parts = exchange(row_sums, PROTOS)
        if step < ITERS - 1:
            col_sums = on_chip(
                functools.partial(col_body, row_count),
                copies_protos,
                (kernel, row_parts),
                work,
                2 * work,
            )
            col_parts = exchange(col_sums, ROWS)
    codes = on_chip(
        functools.partial(codes_body, row_count, row_count * proto_count),
        jax.ShapeDtypeStruct(kernel.shape, jnp.bfloat16),
        (kernel, row_parts, col_scale),
        work,
        3 * work,
    )
    feature_width = embeddings.shape[1]
    term = lax.dot_general(
        codes, embeddings, (((0,), (0,)), ((), ())), preferred_element_type=jnp.float32
    ).astype(jnp.bfloat16)
    near = exchange(term.reshape(count(NEAR), -1, feature_width), NEAR)
    near = jnp.sum(near.astype(jnp.float32), axis=0).astype(jnp.bfloat16)
    sums = jnp.sum(everyone(near, FAR).astype(jnp.float32), axis=0)
    squares = jnp.sum(sums * sums, axis=1, keepdims=True)
    scaled = (sums / jnp.sqrt(squares / feature_width + 1e-06)).astype(jnp.bfloat16)
    return (codes, everyone(scaled, NEAR).reshape(prototypes.shape))


def solution(mesh):
    fine = Mesh(mesh.devices.reshape(tuple(SIZES.values())), tuple(SIZES))
    return jax.shard_map(
        body,
        mesh=fine,
        in_specs=(P(ROWS, None), P(PROTOS, None)),
        out_specs=(P(ROWS, PROTOS), P(PROTOS, None)),
        check_vma=False,
    )
```

```python
import functools

import jax
import jax.numpy as jnp
from jax import lax
from jax.experimental import pallas as pl
from jax.experimental.pallas import tpu as pltpu
from jax.sharding import Mesh, PartitionSpec as P

ITERS = 3
LANES = 128
ROWS = ("ylo", "zhi", "zlo", "x")
PROTOS = ("yhi", "core")
NEAR = ("ylo", "zlo", "x")
FAR = ("zhi",)
SIZES = {"ylo": 2, "zhi": 4, "zlo": 2, "x": 4, "yhi": 4, "core": 2}


def count(axes):
    total = 1
    for axis in axes:
        total *= SIZES[axis]
    return total


def exchange(blocks, axes):
    return lax.all_to_all(blocks, axes, 0, 0, tiled=True)


def everyone(block, axes):
    return exchange(jnp.broadcast_to(block[None], (count(axes), *block.shape)), axes)


def on_chip(body, out_shape, operands, flops, moved):
    spec = pl.BlockSpec(memory_space=pltpu.VMEM)
    return pl.pallas_call(
        body,
        out_shape=out_shape,
        in_specs=[spec] * len(operands),
        out_specs=jax.tree.map(lambda _: spec, out_shape),
        compiler_params=pltpu.CompilerParams(vmem_limit_bytes=40 * 1024 * 1024),
        cost_estimate=pl.CostEstimate(flops=flops, bytes_accessed=moved, transcendentals=0),
    )(*operands)


def blocks_of(size):
    return [slice(start, start + LANES) for start in range(0, size, LANES)]


def down_rows(line):
    return jnp.broadcast_to(line, (LANES, LANES)).T


def load_body(halves, rows_in, protos_in, rows_ref, protos_ref, rows_inv, protos_inv, sems):
    steps = []
    for which, (source, target, inverse) in enumerate(
        ((rows_in, rows_ref, rows_inv), (protos_in, protos_ref, protos_inv))
    ):
        size = source.shape[0] // halves
        for half in range(halves):
            part = pl.ds(half * size, size)
            copy = pltpu.make_async_copy(
                source.at[part, :], target.at[part, :], sems.at[which * halves + half]
            )
            copy.start()
            lines = range(half * size // LANES, (half + 1) * size // LANES)
            steps.append((copy, target, inverse, lines))
    for copy, target, inverse, lines in steps:
        copy.wait()
        for line in lines:
            rows = slice(line * LANES, (line + 1) * LANES)
            total = None
            for lanes in blocks_of(target.shape[1]):
                tile = target[rows, lanes].astype(jnp.float32)
                total = tile * tile if total is None else total + tile * tile
            square = jnp.sum(total.T, axis=0, keepdims=True)
            inverse[line : line + 1, :] = 1.0 / jnp.sqrt(square + 1e-06)


def load(embeddings, prototypes):
    halves = 2
    vmem = pl.BlockSpec(memory_space=pltpu.VMEM)
    whole = pl.BlockSpec(memory_space=pl.ANY)
    arrays = (embeddings, prototypes)
    return pl.pallas_call(
        functools.partial(load_body, halves),
        out_shape=(
            *(jax.ShapeDtypeStruct(a.shape, a.dtype) for a in arrays),
            *(jax.ShapeDtypeStruct((a.shape[0] // LANES, LANES), jnp.float32) for a in arrays),
        ),
        in_specs=[whole, whole],
        out_specs=(vmem,) * 4,
        scratch_shapes=[pltpu.SemaphoreType.DMA((2 * halves,))],
        compiler_params=pltpu.CompilerParams(vmem_limit_bytes=40 * 1024 * 1024),
        cost_estimate=pl.CostEstimate(
            flops=4 * embeddings.size, bytes_accessed=8 * embeddings.size, transcendentals=0
        ),
    )(*arrays)


def send(lines, out_ref):
    block = jnp.concatenate(lines, axis=0).astype(out_ref.dtype)
    out_ref[...] = jnp.broadcast_to(block[None], out_ref.shape)


def row_body(scale, kernel_ref, parts_ref, out_ref):
    col_scale = 1.0 / (scale * jnp.sum(parts_ref[...].astype(jnp.float32), axis=0))
    lines = []
    for rows in blocks_of(kernel_ref.shape[0]):
        total = None
        for k, lanes in enumerate(blocks_of(kernel_ref.shape[1])):
            tile = kernel_ref[rows, lanes] * col_scale[k : k + 1, :]
            total = tile if total is None else total + tile
        lines.append(jnp.sum(total.T, axis=0, keepdims=True))
    send(lines, out_ref)


def col_body(scale, kernel_ref, parts_ref, out_ref):
    row_scale = 1.0 / (scale * jnp.sum(parts_ref[...], axis=0))
    totals = [None] * (kernel_ref.shape[1] // LANES)
    for r, rows in enumerate(blocks_of(kernel_ref.shape[0])):
        turned = down_rows(row_scale[r : r + 1, :])
        for k, lanes in enumerate(blocks_of(kernel_ref.shape[1])):
            tile = kernel_ref[rows, lanes] * turned
            part = jnp.sum(tile.reshape(LANES // 8, 8, LANES), axis=0)
            totals[k] = part if totals[k] is None else totals[k] + part
    lines = [jnp.sum(total, axis=0, keepdims=True) for total in totals]
    send(lines, out_ref)


def unit(values, inverse):
    return (values.astype(jnp.float32) * inverse.reshape(-1, 1)).astype(jnp.bfloat16)


def body(embeddings, prototypes):
    rows, protos = embeddings.shape[0], prototypes.shape[0]
    row_count = float(rows * count(ROWS))
    proto_count = float(protos * count(PROTOS))
    embeddings, prototypes, row_inverse, proto_inverse = load(embeddings, prototypes)
    dots = jnp.dot(
        unit(embeddings, row_inverse),
        unit(prototypes, proto_inverse).T,
        preferred_element_type=jnp.float32,
    )
    kernel = jnp.exp(dots / 0.05)
    line_rows = (rows // LANES, LANES)
    line_protos = (protos // LANES, LANES)
    work = 2 * rows * protos
    first = jnp.sum(kernel, axis=0).reshape(line_protos).astype(jnp.bfloat16)
    col_parts = everyone(first, ROWS)
    for step in range(ITERS):
        row_sums = on_chip(
            functools.partial(row_body, proto_count),
            jax.ShapeDtypeStruct((count(PROTOS), *line_rows), jnp.float32),
            (kernel, col_parts),
            work,
            2 * work,
        )
        row_parts = exchange(row_sums, PROTOS)
        if step < ITERS - 1:
            kind = jnp.float32 if step == ITERS - 2 else jnp.bfloat16
            col_sums = on_chip(
                functools.partial(col_body, row_count),
                jax.ShapeDtypeStruct((count(ROWS), *line_protos), kind),
                (kernel, row_parts),
                work,
                2 * work,
            )
            col_parts = exchange(col_sums, ROWS)
    col_scale = (1.0 / (proto_count * jnp.sum(col_parts, axis=0))).reshape(1, protos)
    row_scale = (1.0 / (row_count * jnp.sum(row_parts, axis=0))).reshape(rows, 1)
    codes = (row_count * proto_count * row_scale * kernel * col_scale).astype(jnp.bfloat16)
    feature_width = embeddings.shape[1]
    term = lax.dot_general(
        codes, embeddings, (((0,), (0,)), ((), ())), preferred_element_type=jnp.float32
    ).astype(jnp.bfloat16)
    near = exchange(term.reshape(count(NEAR), -1, feature_width), NEAR)
    near = jnp.sum(near.astype(jnp.float32), axis=0).astype(jnp.bfloat16)
    sums = jnp.sum(everyone(near, FAR).astype(jnp.float32), axis=0)
    squares = jnp.sum(sums * sums, axis=1, keepdims=True)
    scaled = (sums / jnp.sqrt(squares / feature_width + 1e-06)).astype(jnp.bfloat16)
    return (codes, everyone(scaled, NEAR).reshape(protos, feature_width))


def solution(mesh):
    fine = Mesh(mesh.devices.reshape(tuple(SIZES.values())), tuple(SIZES))
    return jax.shard_map(
        body,
        mesh=fine,
        in_specs=(P(ROWS, None), P(PROTOS, None)),
        out_specs=(P(ROWS, PROTOS), P(PROTOS, None)),
        check_vma=False,
    )
```

```python
import functools

import jax
import jax.numpy as jnp
from jax import lax
from jax.experimental import pallas as pl
from jax.experimental.pallas import tpu as pltpu
from jax.sharding import Mesh, PartitionSpec as P

ITERS = 3
LANES = 128
ROWS = ("ylo", "zhi", "zlo", "x")
PROTOS = ("yhi", "core")
NEAR = ("ylo", "zlo", "x")
FAR = ("zhi",)
SIZES = {"ylo": 2, "zhi": 4, "zlo": 2, "x": 4, "yhi": 4, "core": 2}


def count(axes):
    total = 1
    for axis in axes:
        total *= SIZES[axis]
    return total


def exchange(blocks, axes):
    return lax.all_to_all(blocks, axes, 0, 0, tiled=True)


def everyone(block, axes):
    return exchange(jnp.broadcast_to(block[None], (count(axes), *block.shape)), axes)


def on_chip(body, out_shape, operands, flops, moved):
    spec = pl.BlockSpec(memory_space=pltpu.VMEM)
    return pl.pallas_call(
        body,
        out_shape=out_shape,
        in_specs=[spec] * len(operands),
        out_specs=jax.tree.map(lambda _: spec, out_shape),
        compiler_params=pltpu.CompilerParams(vmem_limit_bytes=40 * 1024 * 1024),
        cost_estimate=pl.CostEstimate(flops=flops, bytes_accessed=moved, transcendentals=0),
    )(*operands)


def blocks_of(size):
    return [slice(start, start + LANES) for start in range(0, size, LANES)]


def down_rows(line):
    return jnp.broadcast_to(line, (LANES, LANES)).T


def load_body(halves, rows_in, protos_in, rows_ref, protos_ref, rows_inv, protos_inv, sems):
    steps = []
    for which, (source, target, inverse) in enumerate(
        ((rows_in, rows_ref, rows_inv), (protos_in, protos_ref, protos_inv))
    ):
        size = source.shape[0] // halves
        for half in range(halves):
            part = pl.ds(half * size, size)
            copy = pltpu.make_async_copy(
                source.at[part, :], target.at[part, :], sems.at[which * halves + half]
            )
            copy.start()
            lines = range(half * size // LANES, (half + 1) * size // LANES)
            steps.append((copy, target, inverse, lines))
    for copy, target, inverse, lines in steps:
        copy.wait()
        for line in lines:
            rows = slice(line * LANES, (line + 1) * LANES)
            total = None
            for lanes in blocks_of(target.shape[1]):
                tile = target[rows, lanes].astype(jnp.float32)
                total = tile * tile if total is None else total + tile * tile
            square = jnp.sum(total.T, axis=0, keepdims=True)
            inverse[line : line + 1, :] = 1.0 / jnp.sqrt(square + 1e-06)


def load(embeddings, prototypes):
    halves = 2
    vmem = pl.BlockSpec(memory_space=pltpu.VMEM)
    whole = pl.BlockSpec(memory_space=pl.ANY)
    arrays = (embeddings, prototypes)
    return pl.pallas_call(
        functools.partial(load_body, halves),
        out_shape=(
            *(jax.ShapeDtypeStruct(a.shape, a.dtype) for a in arrays),
            *(jax.ShapeDtypeStruct((a.shape[0] // LANES, LANES), jnp.float32) for a in arrays),
        ),
        in_specs=[whole, whole],
        out_specs=(vmem,) * 4,
        scratch_shapes=[pltpu.SemaphoreType.DMA((2 * halves,))],
        compiler_params=pltpu.CompilerParams(vmem_limit_bytes=48 * 1024 * 1024),
        cost_estimate=pl.CostEstimate(
            flops=4 * embeddings.size, bytes_accessed=8 * embeddings.size, transcendentals=0
        ),
    )(*arrays)


def send(lines, out_ref):
    block = jnp.concatenate(lines, axis=0).astype(out_ref.dtype)
    out_ref[...] = jnp.broadcast_to(block[None], out_ref.shape)


def row_body(scale, kernel_ref, parts_ref, out_ref, *col_ref):
    col_scale = 1.0 / (scale * jnp.sum(parts_ref[...].astype(jnp.float32), axis=0))
    for ref in col_ref:
        ref[...] = col_scale
    lines = []
    for rows in blocks_of(kernel_ref.shape[0]):
        total = None
        for k, lanes in enumerate(blocks_of(kernel_ref.shape[1])):
            tile = kernel_ref[rows, lanes] * col_scale[k : k + 1, :]
            total = tile if total is None else total + tile
        lines.append(jnp.sum(total.T, axis=0, keepdims=True))
    send(lines, out_ref)


def col_body(scale, kernel_ref, parts_ref, out_ref):
    row_scale = 1.0 / (scale * jnp.sum(parts_ref[...], axis=0))
    totals = [None] * (kernel_ref.shape[1] // LANES)
    for r, rows in enumerate(blocks_of(kernel_ref.shape[0])):
        turned = down_rows(row_scale[r : r + 1, :])
        for k, lanes in enumerate(blocks_of(kernel_ref.shape[1])):
            tile = kernel_ref[rows, lanes] * turned
            part = jnp.sum(tile.reshape(LANES // 8, 8, LANES), axis=0)
            totals[k] = part if totals[k] is None else totals[k] + part
    lines = [jnp.sum(total, axis=0, keepdims=True) for total in totals]
    send(lines, out_ref)


def unit(values, inverse):
    return (values.astype(jnp.float32) * inverse.reshape(-1, 1)).astype(jnp.bfloat16)


def body(embeddings, prototypes):
    rows, protos = embeddings.shape[0], prototypes.shape[0]
    row_count = float(rows * count(ROWS))
    proto_count = float(protos * count(PROTOS))
    embeddings, prototypes, row_inverse, proto_inverse = load(embeddings, prototypes)
    dots = jnp.dot(
        unit(embeddings, row_inverse),
        unit(prototypes, proto_inverse).T,
        preferred_element_type=jnp.float32,
    )
    kernel = jnp.exp(dots / 0.05)
    line_rows = (rows // LANES, LANES)
    line_protos = (protos // LANES, LANES)
    work = 2 * rows * protos
    first = jnp.sum(kernel, axis=0).reshape(line_protos).astype(jnp.bfloat16)
    col_parts = everyone(first, ROWS)
    for step in range(ITERS):
        last = step == ITERS - 1
        row_sums, *col_scale = on_chip(
            functools.partial(row_body, proto_count),
            (
                jax.ShapeDtypeStruct((count(PROTOS), *line_rows), jnp.float32),
                *[jax.ShapeDtypeStruct(line_protos, jnp.float32)] * last,
            ),
            (kernel, col_parts),
            work,
            2 * work,
        )
        row_parts = exchange(row_sums, PROTOS)
        if not last:
            kind = jnp.float32 if step == ITERS - 2 else jnp.bfloat16
            col_sums = on_chip(
                functools.partial(col_body, row_count),
                jax.ShapeDtypeStruct((count(ROWS), *line_protos), kind),
                (kernel, row_parts),
                work,
                2 * work,
            )
            col_parts = exchange(col_sums, ROWS)
    col_scale = col_scale[0].reshape(1, protos)
    row_scale = (1.0 / (row_count * jnp.sum(row_parts, axis=0))).reshape(rows, 1)
    codes = (row_count * proto_count * row_scale * kernel * col_scale).astype(jnp.bfloat16)
    feature_width = embeddings.shape[1]
    term = lax.dot_general(
        codes, embeddings, (((0,), (0,)), ((), ())), preferred_element_type=jnp.float32
    ).astype(jnp.bfloat16)
    near = exchange(term.reshape(count(NEAR), -1, feature_width), NEAR)
    near = jnp.sum(near.astype(jnp.float32), axis=0).astype(jnp.bfloat16)
    sums = jnp.sum(everyone(near, FAR).astype(jnp.float32), axis=0)
    squares = jnp.sum(sums * sums, axis=1, keepdims=True)
    scaled = (sums / jnp.sqrt(squares / feature_width + 1e-06)).astype(jnp.bfloat16)
    return (codes, everyone(scaled, NEAR).reshape(protos, feature_width))


def solution(mesh):
    fine = Mesh(mesh.devices.reshape(tuple(SIZES.values())), tuple(SIZES))
    return jax.shard_map(
        body,
        mesh=fine,
        in_specs=(P(ROWS, None), P(PROTOS, None)),
        out_specs=(P(ROWS, PROTOS), P(PROTOS, None)),
        check_vma=False,
    )
```

```python
import functools

import jax
import jax.numpy as jnp
from jax import lax
from jax.experimental import pallas as pl
from jax.experimental.pallas import tpu as pltpu
from jax.sharding import Mesh, PartitionSpec as P

ITERS = 3
LANES = 128
ROWS = ("ylo", "zhi", "zlo", "x")
PROTOS = ("yhi", "core")
NEAR = ("ylo", "zlo", "x")
FAR = ("zhi",)
SIZES = {"ylo": 2, "zhi": 4, "zlo": 2, "x": 4, "yhi": 4, "core": 2}


def count(axes):
    total = 1
    for axis in axes:
        total *= SIZES[axis]
    return total


def exchange(blocks, axes):
    return lax.all_to_all(blocks, axes, 0, 0, tiled=True)


def everyone(block, axes):
    return exchange(jnp.broadcast_to(block[None], (count(axes), *block.shape)), axes)


def on_chip(body, out_shape, operands, flops, moved):
    spec = pl.BlockSpec(memory_space=pltpu.VMEM)
    return pl.pallas_call(
        body,
        out_shape=out_shape,
        in_specs=[spec] * len(operands),
        out_specs=jax.tree.map(lambda _: spec, out_shape),
        compiler_params=pltpu.CompilerParams(vmem_limit_bytes=40 * 1024 * 1024),
        cost_estimate=pl.CostEstimate(flops=flops, bytes_accessed=moved, transcendentals=0),
    )(*operands)


def blocks_of(size):
    return [slice(start, start + LANES) for start in range(0, size, LANES)]


def down_rows(line):
    return jnp.broadcast_to(line, (LANES, LANES)).T


def load_body(halves, rows_in, protos_in, rows_ref, protos_ref, rows_inv, protos_inv, sems):
    steps = []
    for which, (source, target, inverse) in enumerate(
        ((rows_in, rows_ref, rows_inv), (protos_in, protos_ref, protos_inv))
    ):
        size = source.shape[0] // halves
        for half in range(halves):
            part = pl.ds(half * size, size)
            copy = pltpu.make_async_copy(
                source.at[part, :], target.at[part, :], sems.at[which * halves + half]
            )
            copy.start()
            lines = range(half * size // LANES, (half + 1) * size // LANES)
            steps.append((copy, target, inverse, lines))
    for copy, target, inverse, lines in steps:
        copy.wait()
        for line in lines:
            rows = slice(line * LANES, (line + 1) * LANES)
            total = None
            for lanes in blocks_of(target.shape[1]):
                tile = target[rows, lanes].astype(jnp.float32)
                total = tile * tile if total is None else total + tile * tile
            square = jnp.sum(total.T, axis=0, keepdims=True)
            inverse[line : line + 1, :] = 1.0 / jnp.sqrt(square + 1e-06)


def load(embeddings, prototypes):
    halves = 2
    vmem = pl.BlockSpec(memory_space=pltpu.VMEM)
    whole = pl.BlockSpec(memory_space=pl.ANY)
    arrays = (embeddings, prototypes)
    return pl.pallas_call(
        functools.partial(load_body, halves),
        out_shape=(
            *(jax.ShapeDtypeStruct(a.shape, a.dtype) for a in arrays),
            *(jax.ShapeDtypeStruct((a.shape[0] // LANES, LANES), jnp.float32) for a in arrays),
        ),
        in_specs=[whole, whole],
        out_specs=(vmem,) * 4,
        scratch_shapes=[pltpu.SemaphoreType.DMA((2 * halves,))],
        compiler_params=pltpu.CompilerParams(vmem_limit_bytes=48 * 1024 * 1024),
        cost_estimate=pl.CostEstimate(
            flops=4 * embeddings.size, bytes_accessed=8 * embeddings.size, transcendentals=0
        ),
    )(*arrays)


def send(lines, out_ref):
    block = jnp.concatenate(lines, axis=0).astype(out_ref.dtype)
    out_ref[...] = jnp.broadcast_to(block[None], out_ref.shape)


def row_body(scale, kernel_ref, parts_ref, out_ref, *col_ref):
    col_scale = 1.0 / (scale * jnp.sum(parts_ref[...].astype(jnp.float32), axis=0))
    for ref in col_ref:
        ref[...] = col_scale
    lines = []
    for rows in blocks_of(kernel_ref.shape[0]):
        total = None
        for k, lanes in enumerate(blocks_of(kernel_ref.shape[1])):
            tile = kernel_ref[rows, lanes] * col_scale[k : k + 1, :]
            total = tile if total is None else total + tile
        lines.append(jnp.sum(total.T, axis=0, keepdims=True))
    send(lines, out_ref)


def col_body(scale, kernel_ref, parts_ref, out_ref):
    row_scale = 1.0 / (scale * jnp.sum(parts_ref[...], axis=0))
    totals = [None] * (kernel_ref.shape[1] // LANES)
    for r, rows in enumerate(blocks_of(kernel_ref.shape[0])):
        turned = down_rows(row_scale[r : r + 1, :])
        for k, lanes in enumerate(blocks_of(kernel_ref.shape[1])):
            tile = kernel_ref[rows, lanes] * turned
            part = jnp.sum(tile.reshape(LANES // 8, 8, LANES), axis=0)
            totals[k] = part if totals[k] is None else totals[k] + part
    lines = [jnp.sum(total, axis=0, keepdims=True) for total in totals]
    send(lines, out_ref)


def unit(values, inverse):
    return (values.astype(jnp.float32) * inverse.reshape(-1, 1)).astype(jnp.bfloat16)


def codes_body(scale, mass, kernel_ref, parts_ref, col_ref, codes_ref):
    row_scale = mass / (scale * jnp.sum(parts_ref[...], axis=0))
    col_scale = col_ref[...]
    for r, rows in enumerate(blocks_of(kernel_ref.shape[0])):
        turned = down_rows(row_scale[r : r + 1, :])
        for k, lanes in enumerate(blocks_of(kernel_ref.shape[1])):
            tile = turned * kernel_ref[rows, lanes] * col_scale[k : k + 1, :]
            codes_ref[rows, lanes] = tile.astype(jnp.bfloat16)


def write_body(parts, source, target, sems):
    size = source.shape[0] // parts
    copies = []
    for part in range(parts):
        rows = pl.ds(part * size, size)
        copy = pltpu.make_async_copy(source.at[rows, :], target.at[rows, :], sems.at[part])
        copy.start()
        copies.append(copy)
    for copy in copies:
        copy.wait()


def write_out(array):
    parts = 4
    return pl.pallas_call(
        functools.partial(write_body, parts),
        out_shape=jax.ShapeDtypeStruct(array.shape, array.dtype),
        in_specs=[pl.BlockSpec(memory_space=pltpu.VMEM)],
        out_specs=pl.BlockSpec(memory_space=pl.ANY),
        scratch_shapes=[pltpu.SemaphoreType.DMA((parts,))],
        compiler_params=pltpu.CompilerParams(vmem_limit_bytes=8 * 1024 * 1024),
        cost_estimate=pl.CostEstimate(
            flops=0, bytes_accessed=4 * array.size, transcendentals=0
        ),
    )(array)


def body(embeddings, prototypes):
    rows, protos = embeddings.shape[0], prototypes.shape[0]
    row_count = float(rows * count(ROWS))
    proto_count = float(protos * count(PROTOS))
    embeddings, prototypes, row_inverse, proto_inverse = load(embeddings, prototypes)
    dots = jnp.dot(
        unit(embeddings, row_inverse),
        unit(prototypes, proto_inverse).T,
        preferred_element_type=jnp.float32,
    )
    kernel = jnp.exp(dots / 0.05)
    line_rows = (rows // LANES, LANES)
    line_protos = (protos // LANES, LANES)
    work = 2 * rows * protos
    first = jnp.sum(kernel, axis=0).reshape(line_protos).astype(jnp.bfloat16)
    col_parts = everyone(first, ROWS)
    for step in range(ITERS):
        last = step == ITERS - 1
        row_sums, *col_scale = on_chip(
            functools.partial(row_body, proto_count),
            (
                jax.ShapeDtypeStruct((count(PROTOS), *line_rows), jnp.float32),
                *[jax.ShapeDtypeStruct(line_protos, jnp.float32)] * last,
            ),
            (kernel, col_parts),
            work,
            2 * work,
        )
        row_parts = exchange(row_sums, PROTOS)
        if not last:
            col_sums = on_chip(
                functools.partial(col_body, row_count),
                jax.ShapeDtypeStruct((count(ROWS), *line_protos), jnp.bfloat16),
                (kernel, row_parts),
                work,
                2 * work,
            )
            col_parts = exchange(col_sums, ROWS)
    mass = row_count * proto_count
    early_codes = on_chip(
        functools.partial(codes_body, row_count, mass),
        jax.ShapeDtypeStruct(kernel.shape, jnp.bfloat16),
        (kernel, row_parts, col_scale[0]),
        work,
        3 * work,
    )
    feature_width = embeddings.shape[1]
    term = lax.dot_general(
        early_codes, embeddings, (((0,), (0,)), ((), ())), preferred_element_type=jnp.float32
    ).astype(jnp.bfloat16)
    term, early_codes = lax.optimization_barrier((term, early_codes))
    term, codes = lax.optimization_barrier((term, write_out(early_codes)))
    near = exchange(term.reshape(count(NEAR), -1, feature_width), NEAR)
    near = jnp.sum(near.astype(jnp.float32), axis=0).astype(jnp.bfloat16)
    sums = jnp.sum(everyone(near, FAR).astype(jnp.float32), axis=0)
    squares = jnp.sum(sums * sums, axis=1, keepdims=True)
    scaled = (sums / jnp.sqrt(squares / feature_width + 1e-06)).astype(jnp.bfloat16)
    return (codes, everyone(scaled, NEAR).reshape(protos, feature_width))


def solution(mesh):
    fine = Mesh(mesh.devices.reshape(tuple(SIZES.values())), tuple(SIZES))
    return jax.shard_map(
        body,
        mesh=fine,
        in_specs=(P(ROWS, None), P(PROTOS, None)),
        out_specs=(P(ROWS, PROTOS), P(PROTOS, None)),
        check_vma=False,
    )
```

```python
import functools

import jax
import jax.numpy as jnp
from jax import lax
from jax.experimental import pallas as pl
from jax.experimental.pallas import tpu as pltpu
from jax.sharding import Mesh, PartitionSpec as P

ITERS = 3
LANES = 128
ROWS = ("ylo", "zhi", "zlo", "x")
PROTOS = ("yhi", "core")
NEAR = ("x", "zlo", "ylo")
FAR = ("zhi",)
SIZES = {"ylo": 2, "zhi": 4, "zlo": 2, "x": 4, "yhi": 4, "core": 2}


def count(axes):
    total = 1
    for axis in axes:
        total *= SIZES[axis]
    return total


def exchange(blocks, axes):
    return lax.all_to_all(blocks, axes, 0, 0, tiled=True)


def everyone(block, axes):
    return exchange(jnp.broadcast_to(block[None], (count(axes), *block.shape)), axes)


def on_chip(body, out_shape, operands, flops, moved):
    spec = pl.BlockSpec(memory_space=pltpu.VMEM)
    return pl.pallas_call(
        body,
        out_shape=out_shape,
        in_specs=[spec] * len(operands),
        out_specs=jax.tree.map(lambda _: spec, out_shape),
        compiler_params=pltpu.CompilerParams(vmem_limit_bytes=40 * 1024 * 1024),
        cost_estimate=pl.CostEstimate(flops=flops, bytes_accessed=moved, transcendentals=0),
    )(*operands)


def blocks_of(size):
    return [slice(start, start + LANES) for start in range(0, size, LANES)]


def down_rows(line):
    return jnp.broadcast_to(line, (LANES, LANES)).T


def load_body(halves, rows_in, protos_in, rows_ref, protos_ref, rows_inv, protos_inv, sems):
    steps = []
    for which, (source, target, inverse) in enumerate(
        ((rows_in, rows_ref, rows_inv), (protos_in, protos_ref, protos_inv))
    ):
        size = source.shape[0] // halves
        for half in range(halves):
            part = pl.ds(half * size, size)
            copy = pltpu.make_async_copy(
                source.at[part, :], target.at[part, :], sems.at[which * halves + half]
            )
            copy.start()
            lines = range(half * size // LANES, (half + 1) * size // LANES)
            steps.append((copy, target, inverse, lines))
    for copy, target, inverse, lines in steps:
        copy.wait()
        for line in lines:
            rows = slice(line * LANES, (line + 1) * LANES)
            total = None
            for lanes in blocks_of(target.shape[1]):
                tile = target[rows, lanes].astype(jnp.float32)
                total = tile * tile if total is None else total + tile * tile
            square = jnp.sum(total.T, axis=0, keepdims=True)
            inverse[line : line + 1, :] = 1.0 / jnp.sqrt(square + 1e-06)


def load(embeddings, prototypes):
    halves = 2
    vmem = pl.BlockSpec(memory_space=pltpu.VMEM)
    whole = pl.BlockSpec(memory_space=pl.ANY)
    arrays = (embeddings, prototypes)
    return pl.pallas_call(
        functools.partial(load_body, halves),
        out_shape=(
            *(jax.ShapeDtypeStruct(a.shape, a.dtype) for a in arrays),
            *(jax.ShapeDtypeStruct((a.shape[0] // LANES, LANES), jnp.float32) for a in arrays),
        ),
        in_specs=[whole, whole],
        out_specs=(vmem,) * 4,
        scratch_shapes=[pltpu.SemaphoreType.DMA((2 * halves,))],
        compiler_params=pltpu.CompilerParams(vmem_limit_bytes=48 * 1024 * 1024),
        cost_estimate=pl.CostEstimate(
            flops=4 * embeddings.size, bytes_accessed=8 * embeddings.size, transcendentals=0
        ),
    )(*arrays)


def send(lines, out_ref):
    block = jnp.concatenate(lines, axis=0).astype(out_ref.dtype)
    out_ref[...] = jnp.broadcast_to(block[None], out_ref.shape)


def row_body(scale, kernel_ref, parts_ref, out_ref, *col_ref):
    col_scale = 1.0 / (scale * jnp.sum(parts_ref[...].astype(jnp.float32), axis=0))
    for ref in col_ref:
        ref[...] = col_scale
    lines = []
    for rows in blocks_of(kernel_ref.shape[0]):
        total = None
        for k, lanes in enumerate(blocks_of(kernel_ref.shape[1])):
            tile = kernel_ref[rows, lanes] * col_scale[k : k + 1, :]
            total = tile if total is None else total + tile
        lines.append(jnp.sum(total.T, axis=0, keepdims=True))
    send(lines, out_ref)


def col_body(scale, kernel_ref, parts_ref, out_ref):
    row_scale = 1.0 / (scale * jnp.sum(parts_ref[...], axis=0))
    totals = [None] * (kernel_ref.shape[1] // LANES)
    for r, rows in enumerate(blocks_of(kernel_ref.shape[0])):
        turned = down_rows(row_scale[r : r + 1, :])
        for k, lanes in enumerate(blocks_of(kernel_ref.shape[1])):
            tile = kernel_ref[rows, lanes] * turned
            part = jnp.sum(tile.reshape(LANES // 8, 8, LANES), axis=0)
            totals[k] = part if totals[k] is None else totals[k] + part
    lines = [jnp.sum(total, axis=0, keepdims=True) for total in totals]
    send(lines, out_ref)


def unit(values, inverse):
    return (values.astype(jnp.float32) * inverse.reshape(-1, 1)).astype(jnp.bfloat16)


def codes_body(scale, mass, kernel_ref, parts_ref, col_ref, codes_ref):
    row_scale = mass / (scale * jnp.sum(parts_ref[...], axis=0))
    col_scale = col_ref[...]
    for r, rows in enumerate(blocks_of(kernel_ref.shape[0])):
        turned = down_rows(row_scale[r : r + 1, :])
        for k, lanes in enumerate(blocks_of(kernel_ref.shape[1])):
            tile = turned * kernel_ref[rows, lanes] * col_scale[k : k + 1, :]
            codes_ref[rows, lanes] = tile.astype(jnp.bfloat16)


def write_body(parts, source, target, sems):
    size = source.shape[0] // parts
    copies = []
    for part in range(parts):
        rows = pl.ds(part * size, size)
        copy = pltpu.make_async_copy(source.at[rows, :], target.at[rows, :], sems.at[part])
        copy.start()
        copies.append(copy)
    for copy in copies:
        copy.wait()


def write_out(array):
    parts = 4
    return pl.pallas_call(
        functools.partial(write_body, parts),
        out_shape=jax.ShapeDtypeStruct(array.shape, array.dtype),
        in_specs=[pl.BlockSpec(memory_space=pltpu.VMEM)],
        out_specs=pl.BlockSpec(memory_space=pl.ANY),
        scratch_shapes=[pltpu.SemaphoreType.DMA((parts,))],
        compiler_params=pltpu.CompilerParams(vmem_limit_bytes=8 * 1024 * 1024),
        cost_estimate=pl.CostEstimate(
            flops=0, bytes_accessed=4 * array.size, transcendentals=0
        ),
    )(array)


def body(embeddings, prototypes):
    rows, protos = embeddings.shape[0], prototypes.shape[0]
    row_count = float(rows * count(ROWS))
    proto_count = float(protos * count(PROTOS))
    embeddings, prototypes, row_inverse, proto_inverse = load(embeddings, prototypes)
    dots = jnp.dot(
        unit(embeddings, row_inverse),
        unit(prototypes, proto_inverse).T,
        preferred_element_type=jnp.float32,
    )
    kernel = jnp.exp(dots / 0.05)
    line_rows = (rows // LANES, LANES)
    line_protos = (protos // LANES, LANES)
    work = 2 * rows * protos
    first = jnp.sum(kernel, axis=0).reshape(line_protos).astype(jnp.bfloat16)
    col_parts = everyone(first, ROWS)
    for step in range(ITERS):
        last = step == ITERS - 1
        row_sums, *col_scale = on_chip(
            functools.partial(row_body, proto_count),
            (
                jax.ShapeDtypeStruct((count(PROTOS), *line_rows), jnp.float32),
                *[jax.ShapeDtypeStruct(line_protos, jnp.float32)] * last,
            ),
            (kernel, col_parts),
            work,
            2 * work,
        )
        row_parts = exchange(row_sums, PROTOS)
        if not last:
            col_sums = on_chip(
                functools.partial(col_body, row_count),
                jax.ShapeDtypeStruct((count(ROWS), *line_protos), jnp.bfloat16),
                (kernel, row_parts),
                work,
                2 * work,
            )
            col_parts = exchange(col_sums, ROWS)
    mass = row_count * proto_count
    early_codes = on_chip(
        functools.partial(codes_body, row_count, mass),
        jax.ShapeDtypeStruct(kernel.shape, jnp.bfloat16),
        (kernel, row_parts, col_scale[0]),
        work,
        3 * work,
    )
    feature_width = embeddings.shape[1]
    term = lax.dot_general(
        early_codes, embeddings, (((0,), (0,)), ((), ())), preferred_element_type=jnp.float32
    ).astype(jnp.bfloat16)
    term, early_codes = lax.optimization_barrier((term, early_codes))
    term, codes = lax.optimization_barrier((term, write_out(early_codes)))
    near = exchange(term.reshape(count(NEAR), -1, feature_width), NEAR)
    near = jnp.sum(near.astype(jnp.float32), axis=0).astype(jnp.bfloat16)
    sums = jnp.sum(everyone(near, FAR).astype(jnp.float32), axis=0)
    squares = jnp.sum(sums * sums, axis=1, keepdims=True)
    scaled = (sums / jnp.sqrt(squares / feature_width + 1e-06)).astype(jnp.bfloat16)
    return (codes, everyone(scaled, NEAR).reshape(protos, feature_width))


def solution(mesh):
    fine = Mesh(mesh.devices.reshape(tuple(SIZES.values())), tuple(SIZES))
    return jax.shard_map(
        body,
        mesh=fine,
        in_specs=(P(ROWS, None), P(PROTOS, None)),
        out_specs=(P(ROWS, PROTOS), P(PROTOS, None)),
        check_vma=False,
    )
```

```python
import functools

import jax
import jax.numpy as jnp
from jax import lax
from jax.experimental import pallas as pl
from jax.experimental.pallas import tpu as pltpu
from jax.sharding import Mesh, PartitionSpec as P

ITERS = 3
LANES = 128
ROWS = ("ylo", "zhi", "zlo", "x")
PROTOS = ("yhi", "core")
NEAR = ("x", "zlo", "ylo")
BACK = ("ylo", "zlo", "x")
FAR = ("zhi",)
SIZES = {"ylo": 2, "zhi": 4, "zlo": 2, "x": 4, "yhi": 4, "core": 2}


def count(axes):
    total = 1
    for axis in axes:
        total *= SIZES[axis]
    return total


def exchange(blocks, axes):
    return lax.all_to_all(blocks, axes, 0, 0, tiled=True)


def everyone(block, axes):
    return exchange(jnp.broadcast_to(block[None], (count(axes), *block.shape)), axes)


def on_chip(body, out_shape, operands, flops, moved):
    spec = pl.BlockSpec(memory_space=pltpu.VMEM)
    return pl.pallas_call(
        body,
        out_shape=out_shape,
        in_specs=[spec] * len(operands),
        out_specs=jax.tree.map(lambda _: spec, out_shape),
        compiler_params=pltpu.CompilerParams(vmem_limit_bytes=40 * 1024 * 1024),
        cost_estimate=pl.CostEstimate(flops=flops, bytes_accessed=moved, transcendentals=0),
    )(*operands)


def blocks_of(size):
    return [slice(start, start + LANES) for start in range(0, size, LANES)]


def down_rows(line):
    return jnp.broadcast_to(line, (LANES, LANES)).T


def load_body(halves, rows_in, protos_in, rows_ref, protos_ref, rows_inv, protos_inv, sems):
    steps = []
    for which, (source, target, inverse) in enumerate(
        ((rows_in, rows_ref, rows_inv), (protos_in, protos_ref, protos_inv))
    ):
        size = source.shape[0] // halves
        for half in range(halves):
            part = pl.ds(half * size, size)
            copy = pltpu.make_async_copy(
                source.at[part, :], target.at[part, :], sems.at[which * halves + half]
            )
            copy.start()
            lines = range(half * size // LANES, (half + 1) * size // LANES)
            steps.append((copy, target, inverse, lines))
    for copy, target, inverse, lines in steps:
        copy.wait()
        for line in lines:
            rows = slice(line * LANES, (line + 1) * LANES)
            total = None
            for lanes in blocks_of(target.shape[1]):
                tile = target[rows, lanes].astype(jnp.float32)
                total = tile * tile if total is None else total + tile * tile
            square = jnp.sum(total.T, axis=0, keepdims=True)
            inverse[line : line + 1, :] = 1.0 / jnp.sqrt(square + 1e-06)


def load(embeddings, prototypes):
    halves = 2
    vmem = pl.BlockSpec(memory_space=pltpu.VMEM)
    whole = pl.BlockSpec(memory_space=pl.ANY)
    arrays = (embeddings, prototypes)
    return pl.pallas_call(
        functools.partial(load_body, halves),
        out_shape=(
            *(jax.ShapeDtypeStruct(a.shape, a.dtype) for a in arrays),
            *(jax.ShapeDtypeStruct((a.shape[0] // LANES, LANES), jnp.float32) for a in arrays),
        ),
        in_specs=[whole, whole],
        out_specs=(vmem,) * 4,
        scratch_shapes=[pltpu.SemaphoreType.DMA((2 * halves,))],
        compiler_params=pltpu.CompilerParams(vmem_limit_bytes=48 * 1024 * 1024),
        cost_estimate=pl.CostEstimate(
            flops=4 * embeddings.size, bytes_accessed=8 * embeddings.size, transcendentals=0
        ),
    )(*arrays)


def send(lines, out_ref):
    block = jnp.concatenate(lines, axis=0).astype(out_ref.dtype)
    out_ref[...] = jnp.broadcast_to(block[None], out_ref.shape)


def row_body(scale, kernel_ref, parts_ref, out_ref, *col_ref):
    col_scale = 1.0 / (scale * jnp.sum(parts_ref[...].astype(jnp.float32), axis=0))
    for ref in col_ref:
        ref[...] = col_scale
    lines = []
    for rows in blocks_of(kernel_ref.shape[0]):
        total = None
        for k, lanes in enumerate(blocks_of(kernel_ref.shape[1])):
            tile = kernel_ref[rows, lanes] * col_scale[k : k + 1, :]
            total = tile if total is None else total + tile
        lines.append(jnp.sum(total.T, axis=0, keepdims=True))
    send(lines, out_ref)


def col_body(scale, kernel_ref, parts_ref, out_ref):
    row_scale = 1.0 / (scale * jnp.sum(parts_ref[...], axis=0))
    totals = [None] * (kernel_ref.shape[1] // LANES)
    for r, rows in enumerate(blocks_of(kernel_ref.shape[0])):
        turned = down_rows(row_scale[r : r + 1, :])
        for k, lanes in enumerate(blocks_of(kernel_ref.shape[1])):
            tile = kernel_ref[rows, lanes] * turned
            part = jnp.sum(tile.reshape(LANES // 8, 8, LANES), axis=0)
            totals[k] = part if totals[k] is None else totals[k] + part
    lines = [jnp.sum(total, axis=0, keepdims=True) for total in totals]
    send(lines, out_ref)


def unit(values, inverse):
    return (values.astype(jnp.float32) * inverse.reshape(-1, 1)).astype(jnp.bfloat16)


def codes_body(scale, mass, kernel_ref, parts_ref, col_ref, codes_ref):
    row_scale = mass / (scale * jnp.sum(parts_ref[...], axis=0))
    col_scale = col_ref[...]
    for r, rows in enumerate(blocks_of(kernel_ref.shape[0])):
        turned = down_rows(row_scale[r : r + 1, :])
        for k, lanes in enumerate(blocks_of(kernel_ref.shape[1])):
            tile = turned * kernel_ref[rows, lanes] * col_scale[k : k + 1, :]
            codes_ref[rows, lanes] = tile.astype(jnp.bfloat16)


def write_body(parts, source, target, sems):
    size = source.shape[0] // parts
    copies = []
    for part in range(parts):
        rows = pl.ds(part * size, size)
        copy = pltpu.make_async_copy(source.at[rows, :], target.at[rows, :], sems.at[part])
        copy.start()
        copies.append(copy)
    for copy in copies:
        copy.wait()


def write_out(array):
    parts = 4
    return pl.pallas_call(
        functools.partial(write_body, parts),
        out_shape=jax.ShapeDtypeStruct(array.shape, array.dtype),
        in_specs=[pl.BlockSpec(memory_space=pltpu.VMEM)],
        out_specs=pl.BlockSpec(memory_space=pl.ANY),
        scratch_shapes=[pltpu.SemaphoreType.DMA((parts,))],
        compiler_params=pltpu.CompilerParams(vmem_limit_bytes=8 * 1024 * 1024),
        cost_estimate=pl.CostEstimate(
            flops=0, bytes_accessed=4 * array.size, transcendentals=0
        ),
    )(array)


def body(embeddings, prototypes):
    rows, protos = embeddings.shape[0], prototypes.shape[0]
    row_count = float(rows * count(ROWS))
    proto_count = float(protos * count(PROTOS))
    embeddings, prototypes, row_inverse, proto_inverse = load(embeddings, prototypes)
    dots = jnp.dot(
        unit(embeddings, row_inverse),
        unit(prototypes, proto_inverse).T,
        preferred_element_type=jnp.float32,
    )
    kernel = jnp.exp(dots / 0.05)
    line_rows = (rows // LANES, LANES)
    line_protos = (protos // LANES, LANES)
    work = 2 * rows * protos
    first = jnp.sum(kernel, axis=0).reshape(line_protos).astype(jnp.bfloat16)
    col_parts = everyone(first, ROWS)
    for step in range(ITERS):
        last = step == ITERS - 1
        row_sums, *col_scale = on_chip(
            functools.partial(row_body, proto_count),
            (
                jax.ShapeDtypeStruct((count(PROTOS), *line_rows), jnp.float32),
                *[jax.ShapeDtypeStruct(line_protos, jnp.float32)] * last,
            ),
            (kernel, col_parts),
            work,
            2 * work,
        )
        row_parts = exchange(row_sums, PROTOS)
        if not last:
            col_sums = on_chip(
                functools.partial(col_body, row_count),
                jax.ShapeDtypeStruct((count(ROWS), *line_protos), jnp.bfloat16),
                (kernel, row_parts),
                work,
                2 * work,
            )
            col_parts = exchange(col_sums, ROWS)
    mass = row_count * proto_count
    early_codes = on_chip(
        functools.partial(codes_body, row_count, mass),
        jax.ShapeDtypeStruct(kernel.shape, jnp.bfloat16),
        (kernel, row_parts, col_scale[0]),
        work,
        3 * work,
    )
    feature_width = embeddings.shape[1]
    term = lax.dot_general(
        early_codes, embeddings, (((0,), (0,)), ((), ())), preferred_element_type=jnp.float32
    ).astype(jnp.bfloat16)
    term, early_codes = lax.optimization_barrier((term, early_codes))
    term, codes = lax.optimization_barrier((term, write_out(early_codes)))
    near = exchange(term.reshape(count(NEAR), -1, feature_width), NEAR)
    near = jnp.sum(near.astype(jnp.float32), axis=0).astype(jnp.bfloat16)
    sums = jnp.sum(everyone(near, FAR).astype(jnp.float32), axis=0)
    squares = jnp.sum(sums * sums, axis=1, keepdims=True)
    scaled = (sums / jnp.sqrt(squares / feature_width + 1e-06)).astype(jnp.bfloat16)
    blocks = everyone(scaled, BACK)
    blocks = blocks.reshape(*(SIZES[axis] for axis in BACK), *scaled.shape)
    return (codes, jnp.transpose(blocks, (2, 1, 0, 3, 4)).reshape(protos, feature_width))


def solution(mesh):
    fine = Mesh(mesh.devices.reshape(tuple(SIZES.values())), tuple(SIZES))
    return jax.shard_map(
        body,
        mesh=fine,
        in_specs=(P(ROWS, None), P(PROTOS, None)),
        out_specs=(P(ROWS, PROTOS), P(PROTOS, None)),
        check_vma=False,
    )
```

```python
import functools

import jax
import jax.numpy as jnp
from jax import lax
from jax.experimental import pallas as pl
from jax.experimental.pallas import tpu as pltpu
from jax.sharding import Mesh, PartitionSpec as P

ITERS = 3
LANES = 128
ROWS = ("ylo", "zhi", "zlo", "x")
PROTOS = ("yhi", "core")
NEAR = ("x", "zlo", "ylo")
FAR = ("zhi",)
SIZES = {"ylo": 2, "zhi": 4, "zlo": 2, "x": 4, "yhi": 4, "core": 2}


def count(axes):
    total = 1
    for axis in axes:
        total *= SIZES[axis]
    return total


def exchange(blocks, axes):
    return lax.all_to_all(blocks, axes, 0, 0, tiled=True)


def everyone(block, axes):
    return exchange(jnp.broadcast_to(block[None], (count(axes), *block.shape)), axes)


def on_chip(body, out_shape, operands, flops, moved):
    spec = pl.BlockSpec(memory_space=pltpu.VMEM)
    return pl.pallas_call(
        body,
        out_shape=out_shape,
        in_specs=[spec] * len(operands),
        out_specs=jax.tree.map(lambda _: spec, out_shape),
        compiler_params=pltpu.CompilerParams(vmem_limit_bytes=40 * 1024 * 1024),
        cost_estimate=pl.CostEstimate(flops=flops, bytes_accessed=moved, transcendentals=0),
    )(*operands)


def blocks_of(size):
    return [slice(start, start + LANES) for start in range(0, size, LANES)]


def down_rows(line):
    return jnp.broadcast_to(line, (LANES, LANES)).T


def load_body(halves, rows_in, protos_in, rows_ref, protos_ref, rows_inv, protos_inv, sems):
    steps = []
    for which, (source, target, inverse) in enumerate(
        ((rows_in, rows_ref, rows_inv), (protos_in, protos_ref, protos_inv))
    ):
        size = source.shape[0] // halves
        for half in range(halves):
            part = pl.ds(half * size, size)
            copy = pltpu.make_async_copy(
                source.at[part, :], target.at[part, :], sems.at[which * halves + half]
            )
            copy.start()
            lines = range(half * size // LANES, (half + 1) * size // LANES)
            steps.append((copy, target, inverse, lines))
    for copy, target, inverse, lines in steps:
        copy.wait()
        for line in lines:
            rows = slice(line * LANES, (line + 1) * LANES)
            total = None
            for lanes in blocks_of(target.shape[1]):
                tile = target[rows, lanes].astype(jnp.float32)
                total = tile * tile if total is None else total + tile * tile
            square = jnp.sum(total.T, axis=0, keepdims=True)
            inverse[line : line + 1, :] = 1.0 / jnp.sqrt(square + 1e-06)


def load(embeddings, prototypes):
    halves = 2
    vmem = pl.BlockSpec(memory_space=pltpu.VMEM)
    whole = pl.BlockSpec(memory_space=pl.ANY)
    arrays = (embeddings, prototypes)
    return pl.pallas_call(
        functools.partial(load_body, halves),
        out_shape=(
            *(jax.ShapeDtypeStruct(a.shape, a.dtype) for a in arrays),
            *(jax.ShapeDtypeStruct((a.shape[0] // LANES, LANES), jnp.float32) for a in arrays),
        ),
        in_specs=[whole, whole],
        out_specs=(vmem,) * 4,
        scratch_shapes=[pltpu.SemaphoreType.DMA((2 * halves,))],
        compiler_params=pltpu.CompilerParams(vmem_limit_bytes=48 * 1024 * 1024),
        cost_estimate=pl.CostEstimate(
            flops=4 * embeddings.size, bytes_accessed=8 * embeddings.size, transcendentals=0
        ),
    )(*arrays)


def send(lines, out_ref):
    block = jnp.concatenate(lines, axis=0).astype(out_ref.dtype)
    out_ref[...] = jnp.broadcast_to(block[None], out_ref.shape)


def row_body(scale, kernel_ref, parts_ref, out_ref, *col_ref):
    col_scale = 1.0 / (scale * jnp.sum(parts_ref[...].astype(jnp.float32), axis=0))
    for ref in col_ref:
        ref[...] = col_scale
    lines = []
    for rows in blocks_of(kernel_ref.shape[0]):
        total = None
        for k, lanes in enumerate(blocks_of(kernel_ref.shape[1])):
            tile = kernel_ref[rows, lanes] * col_scale[k : k + 1, :]
            total = tile if total is None else total + tile
        lines.append(jnp.sum(total.T, axis=0, keepdims=True))
    send(lines, out_ref)


def col_body(scale, kernel_ref, parts_ref, out_ref):
    row_scale = 1.0 / (scale * jnp.sum(parts_ref[...].astype(jnp.float32), axis=0))
    totals = [None] * (kernel_ref.shape[1] // LANES)
    for r, rows in enumerate(blocks_of(kernel_ref.shape[0])):
        turned = down_rows(row_scale[r : r + 1, :])
        for k, lanes in enumerate(blocks_of(kernel_ref.shape[1])):
            tile = kernel_ref[rows, lanes] * turned
            part = jnp.sum(tile.reshape(LANES // 8, 8, LANES), axis=0)
            totals[k] = part if totals[k] is None else totals[k] + part
    lines = [jnp.sum(total, axis=0, keepdims=True) for total in totals]
    send(lines, out_ref)


def unit(values, inverse):
    return (values.astype(jnp.float32) * inverse.reshape(-1, 1)).astype(jnp.bfloat16)


def codes_body(scale, mass, kernel_ref, parts_ref, col_ref, codes_ref):
    row_scale = mass / (scale * jnp.sum(parts_ref[...], axis=0))
    col_scale = col_ref[...]
    for r, rows in enumerate(blocks_of(kernel_ref.shape[0])):
        turned = down_rows(row_scale[r : r + 1, :])
        for k, lanes in enumerate(blocks_of(kernel_ref.shape[1])):
            tile = turned * kernel_ref[rows, lanes] * col_scale[k : k + 1, :]
            codes_ref[rows, lanes] = tile.astype(jnp.bfloat16)


def write_body(parts, source, target, sems):
    size = source.shape[0] // parts
    copies = []
    for part in range(parts):
        rows = pl.ds(part * size, size)
        copy = pltpu.make_async_copy(source.at[rows, :], target.at[rows, :], sems.at[part])
        copy.start()
        copies.append(copy)
    for copy in copies:
        copy.wait()


def write_out(array):
    parts = 4
    return pl.pallas_call(
        functools.partial(write_body, parts),
        out_shape=jax.ShapeDtypeStruct(array.shape, array.dtype),
        in_specs=[pl.BlockSpec(memory_space=pltpu.VMEM)],
        out_specs=pl.BlockSpec(memory_space=pl.ANY),
        scratch_shapes=[pltpu.SemaphoreType.DMA((parts,))],
        compiler_params=pltpu.CompilerParams(vmem_limit_bytes=8 * 1024 * 1024),
        cost_estimate=pl.CostEstimate(
            flops=0, bytes_accessed=4 * array.size, transcendentals=0
        ),
    )(array)


def body(embeddings, prototypes):
    rows, protos = embeddings.shape[0], prototypes.shape[0]
    row_count = float(rows * count(ROWS))
    proto_count = float(protos * count(PROTOS))
    embeddings, prototypes, row_inverse, proto_inverse = load(embeddings, prototypes)
    dots = jnp.dot(
        unit(embeddings, row_inverse),
        unit(prototypes, proto_inverse).T,
        preferred_element_type=jnp.float32,
    )
    kernel = jnp.exp(dots / 0.05)
    line_rows = (rows // LANES, LANES)
    line_protos = (protos // LANES, LANES)
    work = 2 * rows * protos
    first = jnp.sum(kernel, axis=0).reshape(line_protos).astype(jnp.bfloat16)
    col_parts = everyone(first, ROWS)
    for step in range(ITERS):
        last = step == ITERS - 1
        row_sums, *col_scale = on_chip(
            functools.partial(row_body, proto_count),
            (
                jax.ShapeDtypeStruct(
                    (count(PROTOS), *line_rows), jnp.float32 if last else jnp.bfloat16
                ),
                *[jax.ShapeDtypeStruct(line_protos, jnp.float32)] * last,
            ),
            (kernel, col_parts),
            work,
            2 * work,
        )
        row_parts = exchange(row_sums, PROTOS)
        if not last:
            col_sums = on_chip(
                functools.partial(col_body, row_count),
                jax.ShapeDtypeStruct((count(ROWS), *line_protos), jnp.bfloat16),
                (kernel, row_parts),
                work,
                2 * work,
            )
            col_parts = exchange(col_sums, ROWS)
    mass = row_count * proto_count
    early_codes = on_chip(
        functools.partial(codes_body, row_count, mass),
        jax.ShapeDtypeStruct(kernel.shape, jnp.bfloat16),
        (kernel, row_parts, col_scale[0]),
        work,
        3 * work,
    )
    feature_width = embeddings.shape[1]
    term = lax.dot_general(
        early_codes, embeddings, (((0,), (0,)), ((), ())), preferred_element_type=jnp.float32
    ).astype(jnp.bfloat16)
    term, early_codes = lax.optimization_barrier((term, early_codes))
    term, codes = lax.optimization_barrier((term, write_out(early_codes)))
    near = exchange(term.reshape(count(NEAR), -1, feature_width), NEAR)
    near = jnp.sum(near.astype(jnp.float32), axis=0).astype(jnp.bfloat16)
    sums = jnp.sum(everyone(near, FAR).astype(jnp.float32), axis=0)
    squares = jnp.sum(sums * sums, axis=1, keepdims=True)
    scaled = (sums / jnp.sqrt(squares / feature_width + 1e-06)).astype(jnp.bfloat16)
    return (codes, everyone(scaled, NEAR).reshape(protos, feature_width))


def solution(mesh):
    fine = Mesh(mesh.devices.reshape(tuple(SIZES.values())), tuple(SIZES))
    return jax.shard_map(
        body,
        mesh=fine,
        in_specs=(P(ROWS, None), P(PROTOS, None)),
        out_specs=(P(ROWS, PROTOS), P(PROTOS, None)),
        check_vma=False,
    )
```

```python
import functools

import jax
import jax.numpy as jnp
from jax import lax
from jax.experimental import pallas as pl
from jax.experimental.pallas import tpu as pltpu
from jax.sharding import Mesh, PartitionSpec as P

ITERS = 3
LANES = 128
ROWS = ("ylo", "zhi", "zlo", "x")
PROTOS = ("yhi", "core")
NEAR = ("x", "zlo", "ylo")
FAR = ("zhi",)
SIZES = {"ylo": 2, "zhi": 4, "zlo": 2, "x": 4, "yhi": 4, "core": 2}


def count(axes):
    total = 1
    for axis in axes:
        total *= SIZES[axis]
    return total


def exchange(blocks, axes):
    return lax.all_to_all(blocks, axes, 0, 0, tiled=True)


def everyone(block, axes):
    return exchange(jnp.broadcast_to(block[None], (count(axes), *block.shape)), axes)


def on_chip(body, out_shape, operands, flops, moved):
    spec = pl.BlockSpec(memory_space=pltpu.VMEM)
    return pl.pallas_call(
        body,
        out_shape=out_shape,
        in_specs=[spec] * len(operands),
        out_specs=jax.tree.map(lambda _: spec, out_shape),
        compiler_params=pltpu.CompilerParams(vmem_limit_bytes=40 * 1024 * 1024),
        cost_estimate=pl.CostEstimate(flops=flops, bytes_accessed=moved, transcendentals=0),
    )(*operands)


def blocks_of(size):
    return [slice(start, start + LANES) for start in range(0, size, LANES)]


def down_rows(line):
    return jnp.broadcast_to(line, (LANES, LANES)).T


def load_body(halves, rows_in, protos_in, rows_ref, protos_ref, rows_inv, protos_inv, sems):
    steps = []
    for which, (source, target, inverse) in enumerate(
        ((rows_in, rows_ref, rows_inv), (protos_in, protos_ref, protos_inv))
    ):
        size = source.shape[0] // halves
        for half in range(halves):
            part = pl.ds(half * size, size)
            copy = pltpu.make_async_copy(
                source.at[part, :], target.at[part, :], sems.at[which * halves + half]
            )
            copy.start()
            lines = range(half * size // LANES, (half + 1) * size // LANES)
            steps.append((copy, target, inverse, lines))
    for copy, target, inverse, lines in steps:
        copy.wait()
        for line in lines:
            rows = slice(line * LANES, (line + 1) * LANES)
            total = None
            for lanes in blocks_of(target.shape[1]):
                tile = target[rows, lanes].astype(jnp.float32)
                total = tile * tile if total is None else total + tile * tile
            square = jnp.sum(total.T, axis=0, keepdims=True)
            inverse[line : line + 1, :] = 1.0 / jnp.sqrt(square + 1e-06)


def load(embeddings, prototypes):
    halves = 2
    vmem = pl.BlockSpec(memory_space=pltpu.VMEM)
    whole = pl.BlockSpec(memory_space=pl.ANY)
    arrays = (embeddings, prototypes)
    return pl.pallas_call(
        functools.partial(load_body, halves),
        out_shape=(
            *(jax.ShapeDtypeStruct(a.shape, a.dtype) for a in arrays),
            *(jax.ShapeDtypeStruct((a.shape[0] // LANES, LANES), jnp.float32) for a in arrays),
        ),
        in_specs=[whole, whole],
        out_specs=(vmem,) * 4,
        scratch_shapes=[pltpu.SemaphoreType.DMA((2 * halves,))],
        compiler_params=pltpu.CompilerParams(vmem_limit_bytes=48 * 1024 * 1024),
        cost_estimate=pl.CostEstimate(
            flops=4 * embeddings.size, bytes_accessed=8 * embeddings.size, transcendentals=0
        ),
    )(*arrays)


def send(lines, out_ref):
    block = jnp.concatenate(lines, axis=0).astype(out_ref.dtype)
    out_ref[...] = jnp.broadcast_to(block[None], out_ref.shape)


def row_body(scale, kernel_ref, parts_ref, out_ref, *col_ref):
    col_scale = 1.0 / (scale * jnp.sum(parts_ref[...].astype(jnp.float32), axis=0))
    for ref in col_ref:
        ref[...] = col_scale
    lines = []
    for rows in blocks_of(kernel_ref.shape[0]):
        total = None
        for k, lanes in enumerate(blocks_of(kernel_ref.shape[1])):
            tile = kernel_ref[rows, lanes] * col_scale[k : k + 1, :]
            total = tile if total is None else total + tile
        lines.append(jnp.sum(total.T, axis=0, keepdims=True))
    send(lines, out_ref)


def col_body(scale, kernel_ref, parts_ref, out_ref):
    row_scale = 1.0 / (scale * jnp.sum(parts_ref[...].astype(jnp.float32), axis=0))
    totals = [None] * (kernel_ref.shape[1] // LANES)
    for r, rows in enumerate(blocks_of(kernel_ref.shape[0])):
        turned = down_rows(row_scale[r : r + 1, :])
        for k, lanes in enumerate(blocks_of(kernel_ref.shape[1])):
            tile = kernel_ref[rows, lanes] * turned
            part = jnp.sum(tile.reshape(LANES // 8, 8, LANES), axis=0)
            totals[k] = part if totals[k] is None else totals[k] + part
    lines = [jnp.sum(total, axis=0, keepdims=True) for total in totals]
    send(lines, out_ref)


def unit(values, inverse):
    return (values.astype(jnp.float32) * inverse.reshape(-1, 1)).astype(jnp.bfloat16)


def codes_body(scale, mass, parts, kernel_ref, parts_ref, col_ref, codes_ref, out_ref, sems):
    row_scale = mass / (scale * jnp.sum(parts_ref[...], axis=0))
    col_scale = col_ref[...]
    size = kernel_ref.shape[0] // parts
    copies = []
    for r, rows in enumerate(blocks_of(kernel_ref.shape[0])):
        turned = down_rows(row_scale[r : r + 1, :])
        for k, lanes in enumerate(blocks_of(kernel_ref.shape[1])):
            tile = turned * kernel_ref[rows, lanes] * col_scale[k : k + 1, :]
            codes_ref[rows, lanes] = tile.astype(jnp.bfloat16)
        if rows.stop % size == 0:
            done = pl.ds(rows.stop - size, size)
            copy = pltpu.make_async_copy(
                codes_ref.at[done, :], out_ref.at[done, :], sems.at[len(copies)]
            )
            copy.start()
            copies.append(copy)
    for copy in copies:
        copy.wait()


def make_codes(scale, mass, kernel, row_parts, col_scale):
    parts = 4
    vmem = pl.BlockSpec(memory_space=pltpu.VMEM)
    shape = jax.ShapeDtypeStruct(kernel.shape, jnp.bfloat16)
    return pl.pallas_call(
        functools.partial(codes_body, scale, mass, parts),
        out_shape=(shape, shape),
        in_specs=[vmem] * 3,
        out_specs=(vmem, pl.BlockSpec(memory_space=pl.ANY)),
        scratch_shapes=[pltpu.SemaphoreType.DMA((parts,))],
        compiler_params=pltpu.CompilerParams(vmem_limit_bytes=40 * 1024 * 1024),
        cost_estimate=pl.CostEstimate(
            flops=2 * kernel.size, bytes_accessed=8 * kernel.size, transcendentals=0
        ),
    )(kernel, row_parts, col_scale)


def body(embeddings, prototypes):
    rows, protos = embeddings.shape[0], prototypes.shape[0]
    row_count = float(rows * count(ROWS))
    proto_count = float(protos * count(PROTOS))
    embeddings, prototypes, row_inverse, proto_inverse = load(embeddings, prototypes)
    dots = jnp.dot(
        unit(embeddings, row_inverse),
        unit(prototypes, proto_inverse).T,
        preferred_element_type=jnp.float32,
    )
    kernel = jnp.exp(dots / 0.05)
    line_rows = (rows // LANES, LANES)
    line_protos = (protos // LANES, LANES)
    work = 2 * rows * protos
    first = jnp.sum(kernel, axis=0).reshape(line_protos).astype(jnp.bfloat16)
    col_parts = everyone(first, ROWS)
    for step in range(ITERS):
        last = step == ITERS - 1
        row_sums, *col_scale = on_chip(
            functools.partial(row_body, proto_count),
            (
                jax.ShapeDtypeStruct(
                    (count(PROTOS), *line_rows), jnp.float32 if last else jnp.bfloat16
                ),
                *[jax.ShapeDtypeStruct(line_protos, jnp.float32)] * last,
            ),
            (kernel, col_parts),
            work,
            2 * work,
        )
        row_parts = exchange(row_sums, PROTOS)
        if not last:
            col_sums = on_chip(
                functools.partial(col_body, row_count),
                jax.ShapeDtypeStruct((count(ROWS), *line_protos), jnp.bfloat16),
                (kernel, row_parts),
                work,
                2 * work,
            )
            col_parts = exchange(col_sums, ROWS)
    mass = row_count * proto_count
    early_codes, codes = make_codes(row_count, mass, kernel, row_parts, col_scale[0])
    feature_width = embeddings.shape[1]
    term = lax.dot_general(
        early_codes, embeddings, (((0,), (0,)), ((), ())), preferred_element_type=jnp.float32
    ).astype(jnp.bfloat16)
    near = exchange(term.reshape(count(NEAR), -1, feature_width), NEAR)
    near = jnp.sum(near.astype(jnp.float32), axis=0).astype(jnp.bfloat16)
    sums = jnp.sum(everyone(near, FAR).astype(jnp.float32), axis=0)
    squares = jnp.sum(sums * sums, axis=1, keepdims=True)
    scaled = (sums / jnp.sqrt(squares / feature_width + 1e-06)).astype(jnp.bfloat16)
    return (codes, everyone(scaled, NEAR).reshape(protos, feature_width))


def solution(mesh):
    fine = Mesh(mesh.devices.reshape(tuple(SIZES.values())), tuple(SIZES))
    return jax.shard_map(
        body,
        mesh=fine,
        in_specs=(P(ROWS, None), P(PROTOS, None)),
        out_specs=(P(ROWS, PROTOS), P(PROTOS, None)),
        check_vma=False,
    )
```

```python
import functools

import jax
import jax.numpy as jnp
from jax import lax
from jax.experimental import pallas as pl
from jax.experimental.pallas import tpu as pltpu
from jax.sharding import Mesh, PartitionSpec as P

ITERS = 3
LANES = 128
ROWS = ("ylo", "zhi", "zlo", "x")
PROTOS = ("yhi", "core")
NEAR = ("x", "zlo", "ylo")
FAR = ("zhi",)
SIZES = {"ylo": 2, "zhi": 4, "zlo": 2, "x": 4, "yhi": 4, "core": 2}


def count(axes):
    total = 1
    for axis in axes:
        total *= SIZES[axis]
    return total


def exchange(blocks, axes):
    return lax.all_to_all(blocks, axes, 0, 0, tiled=True)


def everyone(block, axes):
    return exchange(jnp.broadcast_to(block[None], (count(axes), *block.shape)), axes)


def on_chip(body, out_shape, operands, flops, moved):
    spec = pl.BlockSpec(memory_space=pltpu.VMEM)
    return pl.pallas_call(
        body,
        out_shape=out_shape,
        in_specs=[spec] * len(operands),
        out_specs=jax.tree.map(lambda _: spec, out_shape),
        compiler_params=pltpu.CompilerParams(vmem_limit_bytes=40 * 1024 * 1024),
        cost_estimate=pl.CostEstimate(flops=flops, bytes_accessed=moved, transcendentals=0),
    )(*operands)


def blocks_of(size):
    return [slice(start, start + LANES) for start in range(0, size, LANES)]


def down_rows(line):
    return jnp.broadcast_to(line, (LANES, LANES)).T


def load_body(halves, rows_in, protos_in, rows_ref, protos_ref, rows_inv, protos_inv, sems):
    steps = []
    for which, (source, target, inverse) in enumerate(
        ((rows_in, rows_ref, rows_inv), (protos_in, protos_ref, protos_inv))
    ):
        size = source.shape[0] // halves
        for half in range(halves):
            part = pl.ds(half * size, size)
            copy = pltpu.make_async_copy(
                source.at[part, :], target.at[part, :], sems.at[which * halves + half]
            )
            copy.start()
            lines = range(half * size // LANES, (half + 1) * size // LANES)
            steps.append((copy, target, inverse, lines))
    for copy, target, inverse, lines in steps:
        copy.wait()
        for line in lines:
            rows = slice(line * LANES, (line + 1) * LANES)
            total = None
            for lanes in blocks_of(target.shape[1]):
                tile = target[rows, lanes].astype(jnp.float32)
                total = tile * tile if total is None else total + tile * tile
            square = jnp.sum(total.T, axis=0, keepdims=True)
            inverse[line : line + 1, :] = 1.0 / jnp.sqrt(square + 1e-06)


def load(embeddings, prototypes):
    halves = 2
    vmem = pl.BlockSpec(memory_space=pltpu.VMEM)
    whole = pl.BlockSpec(memory_space=pl.ANY)
    arrays = (embeddings, prototypes)
    return pl.pallas_call(
        functools.partial(load_body, halves),
        out_shape=(
            *(jax.ShapeDtypeStruct(a.shape, a.dtype) for a in arrays),
            *(jax.ShapeDtypeStruct((a.shape[0] // LANES, LANES), jnp.float32) for a in arrays),
        ),
        in_specs=[whole, whole],
        out_specs=(vmem,) * 4,
        scratch_shapes=[pltpu.SemaphoreType.DMA((2 * halves,))],
        compiler_params=pltpu.CompilerParams(vmem_limit_bytes=48 * 1024 * 1024),
        cost_estimate=pl.CostEstimate(
            flops=4 * embeddings.size, bytes_accessed=8 * embeddings.size, transcendentals=0
        ),
    )(*arrays)


def send(lines, out_ref):
    block = jnp.concatenate(lines, axis=0).astype(out_ref.dtype)
    out_ref[...] = jnp.broadcast_to(block[None], out_ref.shape)


def row_body(scale, kernel_ref, parts_ref, out_ref, *col_ref):
    col_scale = 1.0 / (scale * jnp.sum(parts_ref[...].astype(jnp.float32), axis=0))
    for ref in col_ref:
        ref[...] = col_scale
    lines = []
    for rows in blocks_of(kernel_ref.shape[0]):
        total = None
        for k, lanes in enumerate(blocks_of(kernel_ref.shape[1])):
            tile = kernel_ref[rows, lanes] * col_scale[k : k + 1, :]
            total = tile if total is None else total + tile
        lines.append(jnp.sum(total.T, axis=0, keepdims=True))
    send(lines, out_ref)


def col_body(scale, kernel_ref, parts_ref, out_ref):
    row_scale = 1.0 / (scale * jnp.sum(parts_ref[...].astype(jnp.float32), axis=0))
    totals = [None] * (kernel_ref.shape[1] // LANES)
    for r, rows in enumerate(blocks_of(kernel_ref.shape[0])):
        turned = down_rows(row_scale[r : r + 1, :])
        for k, lanes in enumerate(blocks_of(kernel_ref.shape[1])):
            tile = kernel_ref[rows, lanes] * turned
            part = jnp.sum(tile.reshape(LANES // 8, 8, LANES), axis=0)
            totals[k] = part if totals[k] is None else totals[k] + part
    lines = [jnp.sum(total, axis=0, keepdims=True) for total in totals]
    send(lines, out_ref)


def unit(values, inverse):
    return (values.astype(jnp.float32) * inverse.reshape(-1, 1)).astype(jnp.bfloat16)


def codes_body(scale, mass, parts, kernel_ref, parts_ref, col_ref, codes_ref, out_ref, sems):
    row_scale = mass / (scale * jnp.sum(parts_ref[...], axis=0))
    col_scale = col_ref[...]
    size = kernel_ref.shape[0] // parts
    copies = []
    for r, rows in enumerate(blocks_of(kernel_ref.shape[0])):
        turned = down_rows(row_scale[r : r + 1, :])
        for k, lanes in enumerate(blocks_of(kernel_ref.shape[1])):
            tile = turned * kernel_ref[rows, lanes] * col_scale[k : k + 1, :]
            codes_ref[rows, lanes] = tile.astype(jnp.bfloat16)
        if rows.stop % size == 0:
            done = pl.ds(rows.stop - size, size)
            copy = pltpu.make_async_copy(
                codes_ref.at[done, :], out_ref.at[done, :], sems.at[len(copies)]
            )
            copy.start()
            copies.append(copy)
    for copy in copies:
        copy.wait()


def make_codes(scale, mass, kernel, row_parts, col_scale):
    parts = 4
    vmem = pl.BlockSpec(memory_space=pltpu.VMEM)
    shape = jax.ShapeDtypeStruct(kernel.shape, jnp.bfloat16)
    return pl.pallas_call(
        functools.partial(codes_body, scale, mass, parts),
        out_shape=(shape, shape),
        in_specs=[vmem] * 3,
        out_specs=(vmem, pl.BlockSpec(memory_space=pl.ANY)),
        scratch_shapes=[pltpu.SemaphoreType.DMA((parts,))],
        compiler_params=pltpu.CompilerParams(vmem_limit_bytes=40 * 1024 * 1024),
        cost_estimate=pl.CostEstimate(
            flops=2 * kernel.size, bytes_accessed=8 * kernel.size, transcendentals=0
        ),
    )(kernel, row_parts, col_scale)


def center_body(parts_ref, out_ref):
    group = 16
    width = parts_ref.shape[2]
    for start in range(0, parts_ref.shape[1], group):
        rows = slice(start, start + group)
        sums = jnp.sum(parts_ref[:, rows, :].astype(jnp.float32), axis=0)
        squares = jnp.sum(sums * sums, axis=1, keepdims=True)
        scaled = (sums * (1.0 / jnp.sqrt(squares / width + 1e-06))).astype(jnp.bfloat16)
        out_ref[:, rows, :] = jnp.broadcast_to(scaled[None], (out_ref.shape[0], group, width))


def body(embeddings, prototypes):
    rows, protos = embeddings.shape[0], prototypes.shape[0]
    row_count = float(rows * count(ROWS))
    proto_count = float(protos * count(PROTOS))
    embeddings, prototypes, row_inverse, proto_inverse = load(embeddings, prototypes)
    dots = jnp.dot(
        unit(embeddings, row_inverse),
        unit(prototypes, proto_inverse).T,
        preferred_element_type=jnp.float32,
    )
    kernel = jnp.exp(dots / 0.05)
    line_rows = (rows // LANES, LANES)
    line_protos = (protos // LANES, LANES)
    work = 2 * rows * protos
    first = jnp.sum(kernel, axis=0).reshape(line_protos).astype(jnp.bfloat16)
    col_parts = everyone(first, ROWS)
    for step in range(ITERS):
        last = step == ITERS - 1
        row_sums, *col_scale = on_chip(
            functools.partial(row_body, proto_count),
            (
                jax.ShapeDtypeStruct(
                    (count(PROTOS), *line_rows), jnp.float32 if last else jnp.bfloat16
                ),
                *[jax.ShapeDtypeStruct(line_protos, jnp.float32)] * last,
            ),
            (kernel, col_parts),
            work,
            2 * work,
        )
        row_parts = exchange(row_sums, PROTOS)
        if not last:
            col_sums = on_chip(
                functools.partial(col_body, row_count),
                jax.ShapeDtypeStruct((count(ROWS), *line_protos), jnp.bfloat16),
                (kernel, row_parts),
                work,
                2 * work,
            )
            col_parts = exchange(col_sums, ROWS)
    mass = row_count * proto_count
    early_codes, codes = make_codes(row_count, mass, kernel, row_parts, col_scale[0])
    feature_width = embeddings.shape[1]
    term = lax.dot_general(
        early_codes, embeddings, (((0,), (0,)), ((), ())), preferred_element_type=jnp.float32
    ).astype(jnp.bfloat16)
    near = exchange(term.reshape(count(NEAR), -1, feature_width), NEAR)
    near = jnp.sum(near.astype(jnp.float32), axis=0).astype(jnp.bfloat16)
    far = everyone(near, FAR)
    scaled = on_chip(
        center_body,
        jax.ShapeDtypeStruct((count(NEAR), *near.shape), jnp.bfloat16),
        (far,),
        8 * near.size,
        40 * near.size,
    )
    return (codes, exchange(scaled, NEAR).reshape(protos, feature_width))


def solution(mesh):
    fine = Mesh(mesh.devices.reshape(tuple(SIZES.values())), tuple(SIZES))
    return jax.shard_map(
        body,
        mesh=fine,
        in_specs=(P(ROWS, None), P(PROTOS, None)),
        out_specs=(P(ROWS, PROTOS), P(PROTOS, None)),
        check_vma=False,
    )
```
